512 devices in a mesh: section: 8 (over z), expert: 64 (over x, y, core).
Axes of the slice: x: 4, y: 8, z: 8, core: 2. Of those that a mesh axis runs over, the one named last changes fastest.
Arguments:
- held: bfloat16 [8, 256, 5120], P('section', 'expert'), may hold values from -6 to 6
- arrivals: bfloat16 [3, 256, 5120], P(None, 'expert'), may hold values from -6 to 6
- expert_ids: int32 [4, 8, 256, 1], P(None, 'section', 'expert'), may hold values from 0 to 1; in each aligned block of 4 rows (0 to 3, 4 to 7, ..., all dimensions but the last counted through in order) at most 3 rows name the same one
- router_scores: float32 [4, 8, 256], P(None, 'section', 'expert'), may hold values from -6 to 6
- norm_gain: float32 [8, 5120], P('section'), may hold values from 0.25 to 1.75
- w_gate: bfloat16 [8, 5120, 8192], P('section', None, 'expert'), may hold values from -0.078125 to 0.078125
- w_up: bfloat16 [8, 5120, 8192], P('section', None, 'expert'), may hold values from -0.078125 to 0.078125
- w_down: bfloat16 [8, 8192, 5120], P('section', 'expert'), may hold values from -0.09375 to 0.09375
Outputs:
- section_out: bfloat16 [4, 8, 256, 5120], P(None, 'section', 'expert')
The draws below stay inside these ranges and needn't reach their ends.
Inputs may be any that keep to these rules, and one draw needn't show every extreme that they name: `expert_ids`: within the rows of one device (aligned blocks of 4 rows of the flattened leading dimensions) no expert is named by more than 3 rows, a bound that some block reaches.
All inputs are finite; a program needn't handle non-finite values.
Results may differ from the reference program's by a relative error of at most 0.009.
Values may be sent and summed in bfloat16 or wider, within the bound.
A program may use at most 64 MiB of HBM per device.

```python
import math
import jax
import jax.numpy as jnp
import numpy as np
from jax import lax

D = 5120
EW = 4096
FLIGHT = 2
STEPS = 4
TOK_DEV = 4
CAP = 3
UNITS = 128
TOKENS = 256
N_SECTION = 8


def level_of(own_key, dims, pieces, least, top_value):
    def one(position, parts):
        heights = jax.random.uniform(jax.random.fold_in(jax.random.fold_in(own_key, 6), position), (parts,), jnp.float32, least / len(pieces), top_value / len(pieces))
        return jnp.repeat(jnp.exp(heights), dims[position] // parts).reshape((-1,) + (1,) * (len(dims) - position - 1))

    loudness = one(*pieces[0])
    for cut in pieces[1:]:
        loudness = loudness * one(*cut)
    return loudness


def routed_block(own_key, own, number, rows, count, top, limit, slope):
    sequence = jax.random.permutation(own_key, count)
    heavy_load, ordinary = load_shares(count, rows * top, limit, slope, True), load_shares(count, rows * top, limit, slope, False)
    places = jnp.arange(count)

    def named(tallies, turn):
        used = int((tallies > 0).sum())
        fixed = max(1, used // 4)
        shifted = fixed + (places - fixed + turn * (used - fixed)) % max(1, count - fixed)
        return jnp.zeros((count,), jnp.int32).at[sequence[jnp.where(places < fixed, places, shifted)]].set(jnp.asarray(tallies, jnp.int32))

    tallies = jnp.where(number % 4 == 0, named(heavy_load, number // 4), named(ordinary, number - number // 4 - 1))
    mixed = jax.random.permutation(jax.random.fold_in(own, 3), count)
    giver, sink = mixed[0:count // 2 * 2:2], mixed[1:count // 2 * 2:2]
    room = jnp.minimum(tallies[giver] - 1, limit - tallies[sink]) // 2
    room = jnp.where((giver == sequence[0]) | (sink == sequence[0]) | (tallies[sink] == 0), 0, jnp.maximum(room, 0))
    shifted = jax.random.randint(jax.random.fold_in(own, 4), (count // 2,), 0, 1 << 20) % (room + 1)
    tallies = tallies.at[giver].add(-shifted).at[sink].add(shifted)
    labels = jnp.searchsorted(jnp.cumsum(tallies), jnp.arange(rows * top), side="right").astype(jnp.int32)
    grid = labels.reshape(top, rows).T
    grid = grid[jax.random.permutation(jax.random.fold_in(own, 1), rows)]
    turn = jax.random.randint(jax.random.fold_in(own, 2), (rows, 1), 0, top)
    return jnp.take_along_axis(grid, (jnp.arange(top)[None, :] + turn) % top, axis=1)


def load_shares(count, total, limit, slope, full):
    loads = [(1 << 20) // math.isqrt(grade ** slope) + 1 for grade in range(1, count + 1)]
    largest = limit if full else min(limit, max(-(-total // count), total * loads[0] // sum(loads)))
    least = 1 if total - largest >= count - 1 else 0
    given, rest = [largest] + [least] * (count - 1), total - largest - least * (count - 1)
    while rest > 0:
        movable = [i for i in range(1, count) if given[i] < largest] or [i for i in range(1, count) if given[i] < limit]
        mass, left = sum([loads[i] for i in movable]), rest
        for i in movable:
            extra = min(limit - given[i], max(1, left * loads[i] // mass), rest)
            given[i] = given[i] + extra
            rest = rest - extra
    return np.array(given)


def centred(key, dims, width, most, cuts=(), dtype=jnp.bfloat16):
    values = width * jax.random.normal(key, dims, jnp.float32)
    if cuts:
        values = values * level_of(key, dims, cuts, -0.22, 0.18)
    return jnp.clip(values, -most, most).astype(dtype)


def setup_inputs(seed: int = 0) -> dict:
    arg_keys = jax.random.split(jax.random.key(seed), 9)
    held = centred(arg_keys[0], (N_SECTION, TOKENS, D), 1.0, 6.0, ((0, 8), (1, 64)))
    arrivals = centred(arg_keys[1], (STEPS - 1, TOKENS, D), 1.0, 6.0, ((1, 64),))
    expert_ids_keys = jax.random.split(jax.random.fold_in(arg_keys[2], 1), STEPS * N_SECTION * TOKENS // TOK_DEV)
    expert_ids_turns = jax.random.permutation(jax.random.fold_in(arg_keys[2], 3), STEPS * N_SECTION * TOKENS // TOK_DEV)
    expert_ids = jax.vmap(lambda own, number: routed_block(jax.random.fold_in(arg_keys[2], 2), own, number, TOK_DEV, FLIGHT, 1, CAP, 2))(expert_ids_keys, expert_ids_turns).reshape((STEPS, N_SECTION, TOKENS, 1))
    router_scores = centred(arg_keys[3], (STEPS, N_SECTION, TOKENS), 2.0, 6.0, ((1, 8), (2, 64)), jnp.float32)
    norm_gain = jnp.clip(1.0 + 0.15 * jax.random.normal(arg_keys[4], (N_SECTION, D), jnp.float32), 0.25, 1.75)
    w_gate = centred(arg_keys[5], (N_SECTION, D, FLIGHT * EW), D ** -0.5, 0.078125, ((0, 8), (2, 64)))
    w_up = centred(arg_keys[6], (N_SECTION, D, FLIGHT * EW), D ** -0.5, 0.078125, ((0, 8), (2, 64)))
    w_down = centred(arg_keys[7], (N_SECTION, FLIGHT * EW, D), EW ** -0.5, 0.09375, ((0, 8), (1, 64)))
    return dict(held=held, arrivals=arrivals, expert_ids=expert_ids, router_scores=router_scores, norm_gain=norm_gain, w_gate=w_gate, w_up=w_up, w_down=w_down)


def normalize(values, gain):
    wide = values.astype(jnp.float32)
    power = lax.optimization_barrier(jnp.mean(wide * wide, axis=-1, keepdims=True))
    return (wide * lax.rsqrt(power + 1e-05) * gain).astype(jnp.bfloat16)

def apply_layer(current, chosen, scores, gain, gate_w, up_w, down_w):
    normed = normalize(current, gain)
    total = jnp.zeros((current.shape[0], current.shape[1]), jnp.float32)
    blocks_per = EW // UNITS
    for which in range(FLIGHT):
        gate_out = jnp.dot(normed, gate_w[:, which * EW:(which + 1) * EW], preferred_element_type=jnp.float32)
        up_out = jnp.dot(normed, up_w[:, which * EW:(which + 1) * EW], preferred_element_type=jnp.float32)
        hidden = (jax.nn.silu(gate_out) * up_out).astype(jnp.bfloat16)
        down_part = down_w[which * EW:(which + 1) * EW]

        def add_block(block, summed):
            start = (block * UNITS).astype(jnp.int32)
            left = lax.dynamic_slice_in_dim(hidden, start, UNITS, 1)
            right = lax.dynamic_slice_in_dim(down_part, start, UNITS, 0)
            partial_out = jnp.dot(left, right, preferred_element_type=jnp.float32).astype(jnp.bfloat16)
            partial_out = lax.optimization_barrier(partial_out)
            return summed + partial_out.astype(jnp.float32)
        summed = lax.fori_loop(jnp.int32(0), jnp.int32(blocks_per), add_block, jnp.zeros_like(total))
        total = total + jnp.where((chosen == which)[:, None], summed, jnp.float32(0.0))
    weight = jax.nn.sigmoid(scores.astype(jnp.float32))
    return (current.astype(jnp.float32) + weight[:, None] * total).astype(jnp.bfloat16)

def reference(held, arrivals, expert_ids, router_scores, norm_gain, w_gate, w_up, w_down):
    current = [held[section_num] for section_num in range(N_SECTION)]
    collected = []
    for step in range(STEPS):
        outputs = []
        for section_num in range(N_SECTION):
            outputs.append(apply_layer(current[section_num], expert_ids[step, section_num, :, 0], router_scores[step, section_num], norm_gain[section_num], w_gate[section_num], w_up[section_num], w_down[section_num]))
        collected.append(jnp.stack(outputs))
        if step + 1 < STEPS:
            current = [arrivals[step]] + outputs[:-1]
    return jnp.stack(collected)
```

```python
import functools

import jax
import jax.numpy as jnp
from jax import lax
from jax.experimental import pallas as pl
from jax.experimental.pallas import tpu as pltpu
from jax.sharding import PartitionSpec as P

MESH = pl.DeviceIdType.MESH
T = 4
NX, NY = 4, 8
D = 5120
HALF = D // 2
Q = HALF // 4
UNITS = 128
DY = (0, 1, -1, 2, -2, 3, -3, 4)
INV = (0, 2, 1, 4, 3, 6, 5, 7)
BATCH = ((0, 1), (1, 2), (3, 2), (5, 3))
BATCH_OF = (0, 1, 1, 2, 2, 3, 3, 3)
F32, BF16 = jnp.float32, jnp.bfloat16


def kernel(
    rows_ref, gain_ref, ids_ref, score_ref, wg_ref, wu_ref, wd_ref, out_ref,
    wgu, wdn, perm, perm_t, cur, nb, zbuf, zsrc, ag, idb, mask, xs, part, exs, exr,
    rs, r1, fr, fs, ysrc, yr,
    w_send, w_recv, w_local, id_send, id_recv, idx_recv,
    s_own, s_x, s_x2, s_ex, s_rs, s_fs, s_y, s_z,
    r_ag, r_x, r_x2, r_ex, r_r1, r_pure, r_sum, r_y, r_yc, r_z,
):
    section = lax.axis_index("section")
    me = lax.axis_index("expert")
    core = me % 2
    py = (me // 2) % NY
    px = me // (2 * NY)

    def at(dx, dy, c):
        return {"expert": (((px + dx + NX) % NX) * NY + (py + dy + NY) % NY) * 2 + c}

    sibling = at(0, 0, 1 - core)

    def send(src, dst, send_sem, recv_sem, device):
        pltpu.make_async_remote_copy(
            src_ref=src, dst_ref=dst, send_sem=send_sem, recv_sem=recv_sem,
            device_id=device, device_id_type=MESH,
        ).start()

    def wait(ref, sem):
        pltpu.make_async_copy(ref, ref, sem).wait()

    mine = pl.multiple_of(core * HALF, HALF)
    other = pl.multiple_of((1 - core) * HALF, HALF)
    unit = pl.multiple_of(core * UNITS, UNITS)
    local = [
        pltpu.make_async_copy(
            wg_ref.at[pl.ds(mine, HALF)], wgu.at[0, :, pl.ds(unit, UNITS)], w_local.at[0]),
        pltpu.make_async_copy(
            wu_ref.at[pl.ds(mine, HALF)], wgu.at[1, :, pl.ds(unit, UNITS)], w_local.at[1]),
        pltpu.make_async_copy(
            wd_ref.at[:, pl.ds(mine, HALF)], wdn.at[pl.ds(unit, UNITS)], w_local.at[2]),
    ]
    for copy in local:
        copy.start()

    barrier = pltpu.get_barrier_semaphore()
    partners = [sibling]
    partners += [at(0, dy, c) for dy in DY[1:] for c in range(2)]
    partners += [at(dx, 0, c) for dx in (1, -1) for c in range(2)]
    partners += [{"section": (section + 1) % 8}, {"section": (section + 7) % 8}]
    for device in partners:
        pl.semaphore_signal(barrier, inc=1, device_id=device, device_id_type=MESH)

    i = lax.broadcasted_iota(jnp.int32, (256, 256), 0)
    j = lax.broadcasted_iota(jnp.int32, (256, 256), 1)
    perm[...] = jnp.where(
        (i // 64 == (j % 16) // 4) & ((i % 64) // 4 == j // 16) & (i % 4 == j % 4), 1.0, 0.0
    ).astype(BF16)
    perm_t[...] = jnp.where(
        (j // 64 == (i % 16) // 4) & ((j % 64) // 4 == i // 16) & (i % 4 == j % 4), 1.0, 0.0
    ).astype(BF16)
    for a in range(2):
        @pl.when(core == a)
        def _():
            idb[a, 0, 0] = ids_ref[...]

    pl.semaphore_wait(barrier, len(partners))

    remote = [
        (wg_ref.at[pl.ds(other, HALF)], wgu.at[0, :, pl.ds(unit, UNITS)]),
        (wu_ref.at[pl.ds(other, HALF)], wgu.at[1, :, pl.ds(unit, UNITS)]),
        (wd_ref.at[:, pl.ds(other, HALF)], wdn.at[pl.ds(unit, UNITS)]),
    ]

    def spread(t, a):
        @pl.when(core == a)
        def _():
            @pl.when((t > 0) & (section > 0))
            def _():
                wait(zbuf.at[t], r_z.at[t])
                cur[...] = zbuf[t].astype(F32)

            @pl.when((t == 0) | (section == 0))
            def _():
                cur[...] = rows_ref[t].astype(F32)

            wide = cur[...]
            power = jnp.broadcast_to(jnp.sum(wide * wide, axis=1, keepdims=True), (32, 128))
            for shift in (4, 8, 16):
                power = power + pltpu.roll(power, shift, 0)
            scale = lax.rsqrt(power[:, :1] * (1.0 / D) + 1e-05)
            normed = (wide * scale * gain_ref[...]).astype(BF16)
            nb[t, 0] = normed[:16]
            nb[t, 1] = normed[16:]
            for slot in range(1, 8):
                for h in range(2):
                    send(nb.at[t, h], ag.at[t, a, 0, INV[slot]], s_own.at[t, 0],
                         r_ag.at[t, a, BATCH_OF[INV[slot]]], at(0, DY[slot], h))
            for h in range(2):
                send(nb.at[t, h], ag.at[t, a, 1, 0], s_own.at[t, 1], r_x.at[t, a, 0, 0], at(1, 0, h))
                send(nb.at[t, h], ag.at[t, a, 2, 0], s_own.at[t, 1], r_x.at[t, a, 1, 0], at(-1, 0, h))
            send(nb.at[t, 1 - core], ag.at[t, a, 0, 0], s_own.at[t, 1], r_ag.at[t, a, 0], sibling)
            ag[t, a, 0, 0] = nb[t, core]

    def along_y(t, a, k):
        first, count = BATCH[k]
        block = ag.at[t, a, 0, pl.ds(first, count)]
        wait(block, r_ag.at[t, a, k])
        send(block, ag.at[t, a, 1, pl.ds(first, count)], s_x.at[t, a, 0], r_x.at[t, a, 0, k], at(1, 0, core))
        send(block, ag.at[t, a, 2, pl.ds(first, count)], s_x.at[t, a, 1], r_x.at[t, a, 1, k], at(-1, 0, core))

    def along_x(t, a, k):
        first, count = BATCH[k]
        low = ag.at[t, a, 1, pl.ds(first, count)]
        high = ag.at[t, a, 2, pl.ds(first, count)]
        wait(low, r_x.at[t, a, 0, k])
        wait(high, r_x.at[t, a, 1, k])
        dst = ag.at[t, a, 3, pl.ds(first, count)]
        if k in (0, 3):
            send(low, dst, s_x2.at[t, a], r_x2.at[t, a], at(1, 0, core))
        else:
            send(high, dst, s_x2.at[t, a], r_x2.at[t, a], at(-1, 0, core))

    def gate_up(t, a):
        wait(ag.at[t, a, 3], r_x2.at[t, a])

        @pl.when(core != a)
        def _():
            wait(ag.at[t, a, 0, 0], r_ag.at[t, a, 0])

        for g in range(2):
            block = ag[t, a, 2 * g:2 * g + 2].reshape(256, Q)
            moved = jnp.dot(perm[...], block, preferred_element_type=F32).astype(BF16)
            for q in range(4):
                xs[a, 64 * g:64 * g + 64, Q * q:Q * q + Q] = moved[64 * q:64 * q + 64]
        for w in range(2):
            value = jnp.dot(xs[a], wgu[w], preferred_element_type=F32)
            part[a, :, 256 * w:256 * w + 256] = value
            exs[t, a, :, 256 * w:256 * w + 256] = value.astype(BF16)
        send(exs.at[t, a], exr.at[t, a], s_ex.at[t, a], r_ex.at[t, a], sibling)

    def down(t, a):
        wait(exr.at[t, a], r_ex.at[t, a])
        gate = part[a, :, :256] + exr[t, a, :, :256].astype(F32)
        up = part[a, :, 256:] + exr[t, a, :, 256:].astype(F32)
        keep = mask[t, a]
        hidden = (gate / (1.0 + jnp.exp(-gate)) * up * jnp.concatenate([keep, keep], axis=1)).astype(BF16)
        result = jnp.dot(hidden, wdn[...], preferred_element_type=F32).astype(BF16)
        for g in (1, 0):
            piece = jnp.concatenate(
                [result[64 * g:64 * g + 64, Q * q:Q * q + Q] for q in range(4)], axis=0)
            moved = jnp.dot(perm_t[...], piece, preferred_element_type=F32).astype(BF16)
            rs[t, a, 2 * g:2 * g + 2] = moved.reshape(2, 8, 16, Q)
            if g == 1:
                send(rs.at[t, a, 3, pl.ds(0, 4)], r1.at[t, a, 0], s_rs.at[t, a, 0], r_r1.at[t, a, 0], at(1, 0, core))
                send(rs.at[t, a, 3, pl.ds(4, 4)], r1.at[t, a, 1], s_rs.at[t, a, 1], r_r1.at[t, a, 1], at(-1, 0, core))
                send(rs.at[t, a, 2, pl.ds(4, 4)], fr.at[t, a, 0, pl.ds(4, 4)], s_rs.at[t, a, 2], r_pure.at[t, a, 0],
                     at(1, 0, core))
            else:
                send(rs.at[t, a, 1, pl.ds(0, 4)], fr.at[t, a, 1, pl.ds(0, 4)], s_rs.at[t, a, 3], r_pure.at[t, a, 1],
                     at(-1, 0, core))

    def back_x(t, a):
        wait(r1.at[t, a, 0], r_r1.at[t, a, 0])
        fs[t, a, 0] = (rs[t, a, 2, 0:4].astype(F32) + r1[t, a, 0].astype(F32)).astype(BF16)
        send(fs.at[t, a, 0], fr.at[t, a, 0, pl.ds(0, 4)], s_fs.at[t, a, 0], r_sum.at[t, a, 0], at(1, 0, core))
        wait(r1.at[t, a, 1], r_r1.at[t, a, 1])
        fs[t, a, 1] = (rs[t, a, 1, 4:8].astype(F32) + r1[t, a, 1].astype(F32)).astype(BF16)
        send(fs.at[t, a, 1], fr.at[t, a, 1, pl.ds(4, 4)], s_fs.at[t, a, 1], r_sum.at[t, a, 1], at(-1, 0, core))

    def back_y(t, a):
        wait(fr.at[t, a, 0, pl.ds(4, 4)], r_pure.at[t, a, 0])
        wait(fr.at[t, a, 1, pl.ds(0, 4)], r_pure.at[t, a, 1])
        wait(fr.at[t, a, 0, pl.ds(0, 4)], r_sum.at[t, a, 0])
        wait(fr.at[t, a, 1, pl.ds(4, 4)], r_sum.at[t, a, 1])
        for slot in (7, 6, 5, 4, 3, 2, 1, 0):
            ysrc[t, a, slot] = (
                rs[t, a, 0, slot].astype(F32) + fr[t, a, 0, slot].astype(F32) + fr[t, a, 1, slot].astype(F32)
            ).astype(BF16)
            if slot:
                send(ysrc.at[t, a, slot], yr.at[t, core, INV[slot]], s_y.at[t, a, 0], r_y.at[t], at(0, DY[slot], a))

        @pl.when(core == a)
        def _():
            yr[t, core, 0] = ysrc[t, a, 0]

        @pl.when(core != a)
        def _():
            send(ysrc.at[t, a, 0], yr.at[t, core, 0], s_y.at[t, a, 1], r_yc.at[t], sibling)

    def finish(t, a):
        @pl.when(core == a)
        def _():
            wait(yr.at[t, 1 - core, 0], r_yc.at[t])
            wait(yr.at[t, :, pl.ds(1, 7)], r_y.at[t])
            weight = 1.0 / (1.0 + jnp.exp(-score_ref[t]))
            for h in range(2):
                total = yr[t, h, 0].astype(F32)
                for slot in range(1, 8):
                    total = total + yr[t, h, slot].astype(F32)
                value = cur[16 * h:16 * h + 16] + weight[16 * h:16 * h + 16, :1] * total
                zsrc[t, 16 * h:16 * h + 16] = value.astype(BF16)

            @pl.when((t < T - 1) & (section < 7))
            def _():
                send(zsrc.at[t], zbuf.at[t + 1], s_z.at[t], r_z.at[t + 1], {"section": (section + 1) % 8})

            out_ref[t] = zsrc[t]

    def masks():
        for a in range(2):
            wait(idb.at[a, 0, pl.ds(1, 7)], id_recv.at[a, 0])

            @pl.when(core != a)
            def _():
                wait(idb.at[a, 0, 0], id_recv.at[a, 1])

            send(idb.at[a, 0], idb.at[a, 1], id_send.at[2 + 3 * a], idx_recv.at[a, 0], at(1, 0, core))
            send(idb.at[a, 0], idb.at[a, 2], id_send.at[3 + 3 * a], idx_recv.at[a, 1], at(-1, 0, core))
        for a in range(2):
            wait(idb.at[a, 1], idx_recv.at[a, 0])
            wait(idb.at[a, 2], idx_recv.at[a, 1])
            send(idb.at[a, 1], idb.at[a, 3], id_send.at[4 + 3 * a], idx_recv.at[a, 2], at(1, 0, core))

    def masks_end():
        expert = (px // (NX // 2)).astype(F32)
        for a in range(2):
            wait(idb.at[a, 3], idx_recv.at[a, 2])
            for g in range(2):
                named = jnp.dot(
                    perm[...], idb[a, 2 * g:2 * g + 2].reshape(256, 128), preferred_element_type=F32)
                for t in range(T):
                    mask[t, a, 64 * g:64 * g + 64] = jnp.where(named[64 * t:64 * t + 64] == expert, 1.0, 0.0)

    def tick(t, first):
        for a in range(2):
            spread(t, a)
        if first:
            for k, (src, dst) in enumerate(remote):
                send(src, dst, w_send.at[k], w_recv.at[k], sibling)
            for a in range(2):
                @pl.when(core == a)
                def _():
                    for slot in range(1, 8):
                        for h in range(2):
                            send(ids_ref, idb.at[a, 0, INV[slot]], id_send.at[0], id_recv.at[a, 0], at(0, DY[slot], h))
                    send(ids_ref, idb.at[a, 0, 0], id_send.at[1], id_recv.at[a, 1], sibling)
        for k in (1, 0, 2, 3):
            for a in range(2):
                if k:
                    along_y(t, a, k)
                else:
                    along_x(t, a, 0)
        if first:
            masks()
        for k in (1, 2, 3):
            for a in range(2):
                along_x(t, a, k)
        if first:
            masks_end()
            for copy in local:
                copy.wait()
            for k, (_, dst) in enumerate(remote):
                wait(dst, w_recv.at[k])
        for stage in (gate_up, down, back_x, back_y, finish):
            for a in range(2):
                stage(t, a)

    tick(0, True)

    def later(t, _):
        tick(t, False)
        return 0

    lax.fori_loop(1, T, later, 0)

    for k, (src, _) in enumerate(remote):
        wait(src, w_send.at[k])
    wait(idb.at[:, 0, pl.ds(0, 7)], id_send.at[0])
    wait(ids_ref, id_send.at[1])
    for a in range(2):
        for k in range(3):
            wait(idb.at[a, k], id_send.at[2 + 3 * a + k])

    def drain(t, _):
        wait(yr.at[t, :, pl.ds(1, 7)], s_own.at[t, 0])
        wait(yr.at[t, 0, pl.ds(0, 5)], s_own.at[t, 1])
        for a in range(2):
            for d in range(2):
                wait(ag.at[t, a, 0, pl.ds(1, 7)], s_x.at[t, a, d])
                wait(fs.at[t, a, d], s_fs.at[t, a, d])
            wait(ag.at[t, a, 3], s_x2.at[t, a])
            wait(exs.at[t, a], s_ex.at[t, a])
            for k in range(4):
                wait(rs.at[t, a, k, pl.ds(0, 4)], s_rs.at[t, a, k])
            wait(ysrc.at[t, a, pl.ds(1, 7)], s_y.at[t, a, 0])

            @pl.when(core != a)
            def _():
                wait(ysrc.at[t, a, 0], s_y.at[t, a, 1])

        @pl.when((t < T - 1) & (section < 7))
        def _():
            wait(zsrc.at[t], s_z.at[t])
        return 0

    lax.fori_loop(0, T, drain, 0)


def per_device(held, arrivals, expert_ids, router_scores, norm_gain, w_gate, w_up, w_down):
    rows = jnp.concatenate([held, arrivals], axis=0).reshape(T, 4, 8, Q)
    rows = rows.transpose(0, 2, 1, 3).reshape(T, 32, Q)
    gain = jnp.repeat(norm_gain[0].reshape(8, Q), 4, axis=0)
    ids = jnp.broadcast_to(expert_ids.reshape(16, 1).astype(BF16), (16, 128))
    scores = jnp.broadcast_to(jnp.tile(router_scores[:, 0], (1, 8))[:, :, None], (T, 32, 128))
    vmem, anywhere = pl.BlockSpec(memory_space=pltpu.VMEM), pl.BlockSpec(memory_space=pl.ANY)
    dma = pltpu.SemaphoreType.DMA
    out = pl.pallas_call(
        kernel,
        out_shape=jax.ShapeDtypeStruct((T, 32, Q), BF16),
        in_specs=[vmem] * 4 + [anywhere] * 3,
        out_specs=vmem,
        scratch_shapes=[
            pltpu.VMEM((2, HALF, 256), BF16),
            pltpu.VMEM((256, HALF), BF16),
            pltpu.VMEM((256, 256), BF16),
            pltpu.VMEM((256, 256), BF16),
            pltpu.VMEM((32, Q), F32),
            pltpu.VMEM((T, 2, 16, Q), BF16),
            pltpu.VMEM((T, 32, Q), BF16),
            pltpu.VMEM((T, 32, Q), BF16),
            pltpu.VMEM((T, 2, 4, 8, 16, Q), BF16),
            pltpu.VMEM((2, 4, 8, 16, 128), BF16),
            pltpu.VMEM((T, 2, 128, 128), F32),
            pltpu.VMEM((2, 128, HALF), BF16),
            pltpu.VMEM((2, 128, 512), F32),
            pltpu.VMEM((T, 2, 128, 512), BF16),
            pltpu.VMEM((T, 2, 128, 512), BF16),
            pltpu.VMEM((T, 2, 4, 8, 16, Q), BF16),
            pltpu.VMEM((T, 2, 2, 4, 16, Q), BF16),
            pltpu.VMEM((T, 2, 2, 8, 16, Q), BF16),
            pltpu.VMEM((T, 2, 2, 4, 16, Q), BF16),
            pltpu.VMEM((T, 2, 8, 16, Q), BF16),
            pltpu.VMEM((T, 2, 8, 16, Q), BF16),
            dma((3,)), dma((3,)), dma((3,)), dma((8,)), dma((2, 2)), dma((2, 3)),
            dma((T, 2)), dma((T, 2, 2)), dma((T, 2)), dma((T, 2)), dma((T, 2, 4)), dma((T, 2, 2)),
            dma((T, 2, 2)), dma((T,)),
            dma((T, 2, 4)), dma((T, 2, 2, 4)), dma((T, 2)), dma((T, 2)), dma((T, 2, 2)), dma((T, 2, 2)),
            dma((T, 2, 2)), dma((T,)), dma((T,)), dma((T,)),
        ],
        compiler_params=pltpu.CompilerParams(
            collective_id=0, has_side_effects=True, vmem_limit_bytes=56 << 20
        ),
        name="relay",
    )(rows, gain, ids, scores, w_gate[0], w_up[0], w_down[0])
    out = out.reshape(T, 8, 4, Q).transpose(0, 2, 1, 3).reshape(T, 1, 4, D)
    return out


def solution(mesh):
    placed = (
        P("section", "expert", None),
        P(None, "expert", None),
        P(None, "section", "expert", None),
        P(None, "section", "expert"),
        P("section", None),
        P("section", None, "expert"),
        P("section", None, "expert"),
        P("section", "expert", None),
    )
    return jax.shard_map(
        per_device,
        mesh=mesh,
        in_specs=placed,
        out_specs=P(None, "section", "expert", None),
        check_vma=False,
    )
```

```python
import functools

import jax
import jax.numpy as jnp
from jax import lax
from jax.experimental import pallas as pl
from jax.experimental.pallas import tpu as pltpu
from jax.sharding import PartitionSpec as P

MESH = pl.DeviceIdType.MESH
T = 4
NX, NY = 4, 8
D = 5120
HALF = D // 2
Q = HALF // 4
UNITS = 128
DY = (0, 1, -1, 2, -2, 3, -3, 4)
INV = (0, 2, 1, 4, 3, 6, 5, 7)
BATCH = ((0, 1), (1, 2), (3, 2), (5, 3))
BATCH_OF = (0, 1, 1, 2, 2, 3, 3, 3)
ORDER = (
    "Asp", "Bd0'", "Bd1'", "Ay1", "Ax0", "Ay2", "Brf'", "Brn'", "Ay3", "Ax1", "Ax2", "Bbf'", "Bbn'", "Ax3",
    "Ag0", "Ag1", "Bfi'", "Bsp", "Ad0", "Ad1", "By1", "Bx0", "By2", "Arf", "Arn", "By3", "Bx1", "Bx2", "Abf",
    "Abn", "Bx3", "Bg0", "Bg1", "Afi",
)
F32, BF16 = jnp.float32, jnp.bfloat16


def kernel(
    held_ref, arrivals_ref, gain_in, ids_in, score_in, wg_ref, wu_ref, wd_ref, out_ref,
    gain_ref, ids_f, ids_ref, score_ref, wgu, wdn, perm, perm_t, cur, nb, zbuf, zsrc, ag, idb, mask, part, exs, exr,
    rs, r1, fr, fs, ysrc, yr,
    w_send, w_recv, w_local, id_send, id_recv, idx_recv,
    s_own, s_x, s_x2, s_ex, s_rs, s_fs, s_y, s_z,
    r_ag, r_x, r_x2, r_ex, r_r1, r_pure, r_sum, r_y, r_yc, r_z,
):
    section = lax.axis_index("section")
    me = lax.axis_index("expert")
    core = me % 2
    py = (me // 2) % NY
    px = me // (2 * NY)

    def at(dx, dy, c):
        return {"expert": (((px + dx + NX) % NX) * NY + (py + dy + NY) % NY) * 2 + c}

    sibling = at(0, 0, 1 - core)

    def send(src, dst, send_sem, recv_sem, device):
        pltpu.make_async_remote_copy(
            src_ref=src, dst_ref=dst, send_sem=send_sem, recv_sem=recv_sem,
            device_id=device, device_id_type=MESH,
        ).start()

    def wait(ref, sem):
        pltpu.make_async_copy(ref, ref, sem).wait()

    mine = pl.multiple_of(core * HALF, HALF)
    other = pl.multiple_of((1 - core) * HALF, HALF)
    unit = pl.multiple_of(core * UNITS, UNITS)
    local = [
        pltpu.make_async_copy(
            wg_ref.at[pl.ds(mine, HALF)], wgu.at[0, :, pl.ds(unit, UNITS)], w_local.at[0]),
        pltpu.make_async_copy(
            wu_ref.at[pl.ds(mine, HALF)], wgu.at[1, :, pl.ds(unit, UNITS)], w_local.at[1]),
        pltpu.make_async_copy(
            wd_ref.at[:, pl.ds(mine, HALF)], wdn.at[pl.ds(unit, UNITS)], w_local.at[2]),
    ]
    for copy in local:
        copy.start()

    barrier = pltpu.get_barrier_semaphore()
    partners = [sibling]
    partners += [at(0, dy, c) for dy in DY[1:] for c in range(2)]
    partners += [at(dx, 0, c) for dx in (1, -1) for c in range(2)] + [at(2, 0, core)]
    partners += [{"section": (section + 1) % 8}, {"section": (section + 7) % 8}]
    for device in partners:
        pl.semaphore_signal(barrier, inc=1, device_id=device, device_id_type=MESH)

    for k in range(8):
        gain_ref[4 * k:4 * k + 4] = jnp.broadcast_to(gain_in[:, Q * k:Q * k + Q], (4, Q))
    for t in range(T):
        for r in range(4):
            ids_f[4 * t + r:4 * t + r + 1] = jnp.broadcast_to(ids_in[t:t + 1, r:r + 1].astype(F32), (1, 128))
            weight = jnp.broadcast_to(1.0 / (1.0 + jnp.exp(-score_in[t:t + 1, r:r + 1])), (1, 128))
            for k in range(8):
                score_ref[t, 4 * k + r:4 * k + r + 1] = weight
    ids_ref[...] = ids_f[...].astype(BF16)

    i = lax.broadcasted_iota(jnp.int32, (256, 256), 0)
    j = lax.broadcasted_iota(jnp.int32, (256, 256), 1)
    perm[...] = jnp.where(
        (i // 64 == (j % 16) // 4) & ((i % 64) // 4 == j // 16) & (i % 4 == j % 4), 1.0, 0.0
    ).astype(BF16)
    perm_t[...] = jnp.where(
        (j // 64 == (i % 16) // 4) & ((j % 64) // 4 == i // 16) & (i % 4 == j % 4), 1.0, 0.0
    ).astype(BF16)
    for a in range(2):
        @pl.when(core == a)
        def _():
            idb[a, 0, 0] = ids_ref[...]

    pl.semaphore_wait(barrier, len(partners))

    remote = [
        (wg_ref.at[pl.ds(other, HALF)], wgu.at[0, :, pl.ds(unit, UNITS)]),
        (wu_ref.at[pl.ds(other, HALF)], wgu.at[1, :, pl.ds(unit, UNITS)]),
        (wd_ref.at[:, pl.ds(other, HALF)], wdn.at[pl.ds(unit, UNITS)]),
    ]

    def place(rows):
        for k in range(8):
            cur[4 * k:4 * k + 4] = rows[:, Q * k:Q * k + Q]

    def spread(t, a):
        @pl.when(core == a)
        def _():
            if not isinstance(t, int):
                @pl.when(section > 0)
                def _():
                    wait(zbuf.at[t], r_z.at[t])
                    cur[...] = zbuf[t].astype(F32)

            if isinstance(t, int):
                place(held_ref[...].astype(F32))
            else:
                @pl.when(section == 0)
                def _():
                    place(arrivals_ref[t - 1].astype(F32))

            wide = cur[...]
            power = jnp.broadcast_to(jnp.sum(wide * wide, axis=1, keepdims=True), (32, 128))
            for shift in (4, 8, 16):
                power = power + pltpu.roll(power, shift, 0)
            scale = lax.rsqrt(power[:, :1] * (1.0 / D) + 1e-05)
            normed = (wide * scale * gain_ref[...]).astype(BF16)
            nb[t, 0] = normed[:16]
            nb[t, 1] = normed[16:]
            for slot in (1, 2):
                for h in range(2):
                    send(nb.at[t, h], ag.at[t, a, 0, INV[slot]], s_own.at[t, 0],
                         r_ag.at[t, a, BATCH_OF[INV[slot]]], at(0, DY[slot], h))
            for h in range(2):
                send(nb.at[t, h], ag.at[t, a, 1, 0], s_own.at[t, 1], r_x.at[t, a, 0, 0], at(1, 0, h))
                send(nb.at[t, h], ag.at[t, a, 2, 0], s_own.at[t, 1], r_x.at[t, a, 1, 0], at(-1, 0, h))
            for slot in range(3, 8):
                for h in range(2):
                    send(nb.at[t, h], ag.at[t, a, 0, INV[slot]], s_own.at[t, 0],
                         r_ag.at[t, a, BATCH_OF[INV[slot]]], at(0, DY[slot], h))
            send(nb.at[t, 1 - core], ag.at[t, a, 0, 0], s_own.at[t, 1], r_ag.at[t, a, 0], sibling)
            ag[t, a, 0, 0] = nb[t, core]

    def along_y(t, a, k):
        first, count = BATCH[k]
        block = ag.at[t, a, 0, pl.ds(first, count)]
        wait(block, r_ag.at[t, a, k])
        send(block, ag.at[t, a, 1, pl.ds(first, count)], s_x.at[t, a, 0], r_x.at[t, a, 0, k], at(1, 0, core))
        send(block, ag.at[t, a, 2, pl.ds(first, count)], s_x.at[t, a, 1], r_x.at[t, a, 1, k], at(-1, 0, core))
        if k == 3:
            send(block, ag.at[t, a, 3, pl.ds(first, count)], s_x2.at[t, a], r_x2.at[t, a], at(2, 0, core))

    def along_x(t, a, k):
        first, count = BATCH[k]
        low = ag.at[t, a, 1, pl.ds(first, count)]
        high = ag.at[t, a, 2, pl.ds(first, count)]
        wait(low, r_x.at[t, a, 0, k])
        wait(high, r_x.at[t, a, 1, k])
        dst = ag.at[t, a, 3, pl.ds(first, count)]
        if k == 0:
            send(low, dst, s_x2.at[t, a], r_x2.at[t, a], at(1, 0, core))
        elif k < 3:
            send(high, dst, s_x2.at[t, a], r_x2.at[t, a], at(-1, 0, core))

    def gate_up(t, a, s):
        if s == 0:
            @pl.when(core != a)
            def _():
                wait(ag.at[t, a, 0, 0], r_ag.at[t, a, 0])
        else:
            wait(ag.at[t, a, 3], r_x2.at[t, a])
        low = 64 * s
        block = ag[t, a, 2 * s:2 * s + 2].reshape(256, Q)
        moved = jnp.dot(perm[...], block, preferred_element_type=F32).astype(BF16)
        rows = jnp.concatenate([moved[64 * q:64 * q + 64] for q in range(4)], axis=1)
        for w in range(2):
            value = jnp.dot(rows, wgu[w], preferred_element_type=F32)
            part[a, low:low + 64, 256 * w:256 * w + 256] = value
            exs[t, a, low:low + 64, 256 * w:256 * w + 256] = value.astype(BF16)
        mine_now = pl.ds(low, 64)
        send(exs.at[t, a, mine_now], exr.at[t, a, mine_now], s_ex.at[t, a, s], r_ex.at[t, a, s], sibling)

    def down(t, a, s):
        low = 64 * s
        wait(exr.at[t, a, pl.ds(low, 64)], r_ex.at[t, a, s])
        sums = part[a, low:low + 64] + exr[t, a, low:low + 64].astype(F32)
        gate, up = sums[:, :256], sums[:, 256:]
        keep = mask[t, a, low:low + 64]
        hidden = (gate / (1.0 + jnp.exp(-gate)) * up * jnp.concatenate([keep, keep], axis=1)).astype(BF16)
        result = jnp.dot(hidden, wdn[...], preferred_element_type=F32).astype(BF16)
        piece = jnp.concatenate([result[:, Q * q:Q * q + Q] for q in range(4)], axis=0)
        moved = jnp.dot(perm_t[...], piece, preferred_element_type=F32).astype(BF16)
        rs[t, a, 2 * s:2 * s + 2] = moved.reshape(2, 8, 16, Q)
        near, far = pl.ds(0, 4), pl.ds(4, 4)
        if s:
            send(rs.at[t, a, 3, far], r1.at[t, a, 1], s_rs.at[t, a, 1], r_r1.at[t, a, 1], at(-1, 0, core))
            send(rs.at[t, a, 3, near], r1.at[t, a, 0], s_rs.at[t, a, 0], r_r1.at[t, a, 0], at(1, 0, core))
            send(rs.at[t, a, 2, far], fr.at[t, a, 0, far], s_rs.at[t, a, 2], r_pure.at[t, a, 0], at(1, 0, core))
        else:
            send(rs.at[t, a, 1, near], fr.at[t, a, 1, near], s_rs.at[t, a, 3], r_pure.at[t, a, 1], at(-1, 0, core))

    def relay(t, a, far):
        low = 4 * far
        here, step = (1, -1) if far else (2, 1)
        wait(r1.at[t, a, far], r_r1.at[t, a, far])
        fs[t, a, far] = (rs[t, a, here, low:low + 4].astype(F32) + r1[t, a, far].astype(F32)).astype(BF16)
        send(fs.at[t, a, far], fr.at[t, a, far, pl.ds(low, 4)], s_fs.at[t, a, far], r_sum.at[t, a, far],
             at(step, 0, core))

    def back_y(t, a, far):
        block = pl.ds(4 * far, 4)
        wait(fr.at[t, a, 1 - far, block], r_pure.at[t, a, 1 - far])
        wait(fr.at[t, a, far, block], r_sum.at[t, a, far])
        for slot in range(4 * far + 3, 4 * far - 1, -1):
            ysrc[t, a, slot] = (
                rs[t, a, 0, slot].astype(F32) + fr[t, a, 0, slot].astype(F32) + fr[t, a, 1, slot].astype(F32)
            ).astype(BF16)
            if slot:
                send(ysrc.at[t, a, slot], yr.at[t, core, INV[slot]], s_y.at[t, a, 0], r_y.at[t], at(0, DY[slot], a))
        if not far:
            @pl.when(core == a)
            def _():
                yr[t, core, 0] = ysrc[t, a, 0]

            @pl.when(core != a)
            def _():
                send(ysrc.at[t, a, 0], yr.at[t, core, 0], s_y.at[t, a, 1], r_yc.at[t], sibling)

    def finish(t, a):
        @pl.when(core == a)
        def _():
            wait(yr.at[t, 1 - core, 0], r_yc.at[t])
            wait(yr.at[t, :, pl.ds(1, 7)], r_y.at[t])
            weight = score_ref[t]
            for h in range(2):
                total = yr[t, h, 0].astype(F32)
                for slot in range(1, 8):
                    total = total + yr[t, h, slot].astype(F32)
                value = cur[16 * h:16 * h + 16] + weight[16 * h:16 * h + 16, :1] * total
                zsrc[t, 16 * h:16 * h + 16] = value.astype(BF16)
                for q in range(4):
                    k = 4 * h + q
                    out_ref[t, :, Q * k:Q * k + Q] = value[4 * q:4 * q + 4].astype(BF16)

            @pl.when((t < T - 1) & (section < 7))
            def _():
                send(zsrc.at[t], zbuf.at[t + 1], s_z.at[t], r_z.at[t + 1], {"section": (section + 1) % 8})

    def masks():
        for a in range(2):
            wait(idb.at[a, 0, pl.ds(1, 7)], id_recv.at[a, 0])

            @pl.when(core != a)
            def _():
                wait(idb.at[a, 0, 0], id_recv.at[a, 1])

            send(idb.at[a, 0], idb.at[a, 1], id_send.at[2 + 3 * a], idx_recv.at[a, 0], at(1, 0, core))
            send(idb.at[a, 0], idb.at[a, 2], id_send.at[3 + 3 * a], idx_recv.at[a, 1], at(-1, 0, core))
        for a in range(2):
            wait(idb.at[a, 1], idx_recv.at[a, 0])
            wait(idb.at[a, 2], idx_recv.at[a, 1])
            send(idb.at[a, 1], idb.at[a, 3], id_send.at[4 + 3 * a], idx_recv.at[a, 2], at(1, 0, core))

    def masks_end():
        expert = (px // (NX // 2)).astype(F32)
        for a in range(2):
            wait(idb.at[a, 3], idx_recv.at[a, 2])
            for g in range(2):
                named = jnp.dot(
                    perm[...], idb[a, 2 * g:2 * g + 2].reshape(256, 128), preferred_element_type=F32)
                for t in range(T):
                    mask[t, a, 64 * g:64 * g + 64] = jnp.where(named[64 * t:64 * t + 64] == expert, 1.0, 0.0)

    def start():
        for k, (src, dst) in enumerate(remote):
            send(src, dst, w_send.at[k], w_recv.at[k], sibling)
        for a in range(2):
            @pl.when(core == a)
            def _():
                for slot in range(1, 8):
                    for h in range(2):
                        send(ids_ref, idb.at[a, 0, INV[slot]], id_send.at[0], id_recv.at[a, 0], at(0, DY[slot], h))
                send(ids_ref, idb.at[a, 0, 0], id_send.at[1], id_recv.at[a, 1], sibling)

    def ready():
        masks()
        masks_end()
        for copy in local:
            copy.wait()
        for k, (_, dst) in enumerate(remote):
            wait(dst, w_recv.at[k])

    stages = {
        "sp": spread, "fi": finish,
        "y1": lambda t, a: along_y(t, a, 1), "y2": lambda t, a: along_y(t, a, 2), "y3": lambda t, a: along_y(t, a, 3),
        "x0": lambda t, a: along_x(t, a, 0), "x1": lambda t, a: along_x(t, a, 1),
        "x2": lambda t, a: along_x(t, a, 2), "x3": lambda t, a: along_x(t, a, 3),
        "g0": lambda t, a: gate_up(t, a, 0), "g1": lambda t, a: gate_up(t, a, 1),
        "d0": lambda t, a: down(t, a, 0), "d1": lambda t, a: down(t, a, 1),
        "rf": lambda t, a: relay(t, a, 1), "rn": lambda t, a: relay(t, a, 0),
        "bf": lambda t, a: back_y(t, a, 1), "bn": lambda t, a: back_y(t, a, 0),
    }

    def tick(t, parts, first=False):
        for name in ORDER:
            late = name.endswith("'")
            if ("late" if late else "now") not in parts:
                continue
            if first and name == "Ag0":
                ready()
            stages[name[1:3]](t - 1 if late else t, "AB".index(name[0]))
            if first and name == "Asp":
                start()

    tick(0, ("now",), first=True)

    def later(t, _):
        tick(t, ("now", "late"))
        return 0

    lax.fori_loop(1, T, later, 0)
    tick(T, ("late",))

    for k, (src, _) in enumerate(remote):
        wait(src, w_send.at[k])
    wait(idb.at[:, 0, pl.ds(0, 7)], id_send.at[0])
    wait(ids_ref, id_send.at[1])
    for a in range(2):
        for k in range(3):
            wait(idb.at[a, k], id_send.at[2 + 3 * a + k])

    def drain(t, _):
        wait(yr.at[t, :, pl.ds(1, 7)], s_own.at[t, 0])
        wait(yr.at[t, 0, pl.ds(0, 5)], s_own.at[t, 1])
        for a in range(2):
            for d in range(2):
                wait(ag.at[t, a, 0, pl.ds(1, 7)], s_x.at[t, a, d])
                wait(fs.at[t, a, d], s_fs.at[t, a, d])
                wait(exs.at[t, a, pl.ds(64 * d, 64)], s_ex.at[t, a, d])
            wait(ag.at[t, a, 3], s_x2.at[t, a])
            for k in range(4):
                wait(rs.at[t, a, k, pl.ds(0, 4)], s_rs.at[t, a, k])
            wait(ysrc.at[t, a, pl.ds(1, 7)], s_y.at[t, a, 0])

            @pl.when(core != a)
            def _():
                wait(ysrc.at[t, a, 0], s_y.at[t, a, 1])

        @pl.when((t < T - 1) & (section < 7))
        def _():
            wait(zsrc.at[t], s_z.at[t])
        return 0

    lax.fori_loop(0, T, drain, 0)


def per_device(held, arrivals, expert_ids, router_scores, norm_gain, w_gate, w_up, w_down):
    vmem, anywhere = pl.BlockSpec(memory_space=pltpu.VMEM), pl.BlockSpec(memory_space=pl.ANY)
    dma = pltpu.SemaphoreType.DMA
    out = pl.pallas_call(
        kernel,
        out_shape=jax.ShapeDtypeStruct((T, 4, D), BF16),
        in_specs=[vmem] * 5 + [anywhere] * 3,
        out_specs=vmem,
        scratch_shapes=[
            pltpu.VMEM((32, Q), F32),
            pltpu.VMEM((16, 128), F32),
            pltpu.VMEM((16, 128), BF16),
            pltpu.VMEM((T, 32, 128), F32),
            pltpu.VMEM((2, HALF, 256), BF16),
            pltpu.VMEM((256, HALF), BF16),
            pltpu.VMEM((256, 256), BF16),
            pltpu.VMEM((256, 256), BF16),
            pltpu.VMEM((32, Q), F32),
            pltpu.VMEM((T, 2, 16, Q), BF16),
            pltpu.VMEM((T, 32, Q), BF16),
            pltpu.VMEM((T, 32, Q), BF16),
            pltpu.VMEM((T, 2, 4, 8, 16, Q), BF16),
            pltpu.VMEM((2, 4, 8, 16, 128), BF16),
            pltpu.VMEM((T, 2, 128, 128), F32),
            pltpu.VMEM((2, 128, 512), F32),
            pltpu.VMEM((T, 2, 128, 512), BF16),
            pltpu.VMEM((T, 2, 128, 512), BF16),
            pltpu.VMEM((T, 2, 4, 8, 16, Q), BF16),
            pltpu.VMEM((T, 2, 2, 4, 16, Q), BF16),
            pltpu.VMEM((T, 2, 2, 8, 16, Q), BF16),
            pltpu.VMEM((T, 2, 2, 4, 16, Q), BF16),
            pltpu.VMEM((T, 2, 8, 16, Q), BF16),
            pltpu.VMEM((T, 2, 8, 16, Q), BF16),
            dma((3,)), dma((3,)), dma((3,)), dma((8,)), dma((2, 2)), dma((2, 3)),
            dma((T, 2)), dma((T, 2, 2)), dma((T, 2)), dma((T, 2, 2)), dma((T, 2, 4)), dma((T, 2, 2)),
            dma((T, 2, 2)), dma((T,)),
            dma((T, 2, 4)), dma((T, 2, 2, 4)), dma((T, 2)), dma((T, 2, 2)), dma((T, 2, 2)), dma((T, 2, 2)),
            dma((T, 2, 2)), dma((T,)), dma((T,)), dma((T,)),
        ],
        compiler_params=pltpu.CompilerParams(
            collective_id=0, has_side_effects=True, vmem_limit_bytes=56 << 20
        ),
        name="relay",
    )(
        held[0], arrivals, norm_gain, expert_ids.reshape(T, 4), router_scores.reshape(T, 4),
        w_gate[0], w_up[0], w_down[0],
    )
    return out.reshape(T, 1, 4, D)


def solution(mesh):
    placed = (
        P("section", "expert", None),
        P(None, "expert", None),
        P(None, "section", "expert", None),
        P(None, "section", "expert"),
        P("section", None),
        P("section", None, "expert"),
        P("section", None, "expert"),
        P("section", "expert", None),
    )
    return jax.shard_map(
        per_device,
        mesh=mesh,
        in_specs=placed,
        out_specs=P(None, "section", "expert", None),
        check_vma=False,
    )
```

```python
import functools

import jax
import jax.numpy as jnp
from jax import lax
from jax.experimental import pallas as pl
from jax.experimental.pallas import tpu as pltpu
from jax.sharding import PartitionSpec as P

MESH = pl.DeviceIdType.MESH
T = 4
NX, NY = 4, 8
D = 5120
HALF = D // 2
Q = HALF // 4
UNITS = 128
DY = (0, 1, -1, 2, -2, 3, -3, 4)
INV = (0, 2, 1, 4, 3, 6, 5, 7)
BATCH = ((0, 1), (1, 2), (3, 2), (5, 3))
BATCH_OF = (0, 1, 1, 2, 2, 3, 3, 3)
ORDER = (
    "Asp", "Bdn'", "Ay1", "Ax0", "Brf'", "Brn'", "Ay2", "Ay3", "Ax1", "Bbf'", "Bbn'",
    "Adr'", "Ax2", "Ax3", "Ag0", "Ag1", "Bfi'", "Bsp", "Adn", "By1", "Bx0", "Arf",
    "Arn", "By2", "By3", "Bx1", "Abf", "Abn", "Bdr'", "Bx2", "Bx3", "Bg0", "Bg1", "Afi",
)
F32, BF16 = jnp.float32, jnp.bfloat16


def kernel(
    held_ref, arrivals_ref, gain_in, ids_in, score_in, wg_ref, wu_ref, wd_ref, out_ref,
    gain_ref, ids_f, ids_ref, score_ref, wgu, wdn, perm, perm_t, cur, nb, zbuf, zsrc, ag, idb, mask, part, exs, exr,
    rs, r1, fr, fs, ysrc, yr,
    w_send, w_recv, w_local, id_send, id_recv, idx_recv,
    s_own, s_x, s_x2, s_ex, s_rs, s_fs, s_y, s_z,
    r_ag, r_x, r_x2, r_ex, r_r1, r_pure, r_sum, r_y, r_yc, r_z,
):
    section = lax.axis_index("section")
    me = lax.axis_index("expert")
    core = lax.rem(me, 2)
    chip = lax.div(me, 2)
    py = lax.rem(chip, NY)
    px = lax.div(chip, NY)
    chips = {(0, dy): (px * NY + lax.rem(py + dy + NY, NY)) * 2 for dy in DY}
    chips.update({(dx, 0): (lax.rem(px + dx + NX, NX) * NY + py) * 2 for dx in (1, -1, 2)})
    above, below = lax.rem(section + 1, 8), lax.rem(section + 7, 8)

    def at(dx, dy, c):
        return {"expert": chips[dx, dy] + c}

    sibling = at(0, 0, 1 - core)

    def send(src, dst, send_sem, recv_sem, device):
        pltpu.make_async_remote_copy(
            src_ref=src, dst_ref=dst, send_sem=send_sem, recv_sem=recv_sem,
            device_id=device, device_id_type=MESH,
        ).start()

    def wait(ref, sem):
        pltpu.make_async_copy(ref, ref, sem).wait()

    mine = pl.multiple_of(core * HALF, HALF)
    other = pl.multiple_of((1 - core) * HALF, HALF)
    unit = pl.multiple_of(core * UNITS, UNITS)
    local = [
        pltpu.make_async_copy(
            wg_ref.at[pl.ds(mine, HALF)], wgu.at[0, :, pl.ds(unit, UNITS)], w_local.at[0]),
        pltpu.make_async_copy(
            wu_ref.at[pl.ds(mine, HALF)], wgu.at[1, :, pl.ds(unit, UNITS)], w_local.at[1]),
        pltpu.make_async_copy(
            wd_ref.at[:, pl.ds(mine, HALF)], wdn.at[pl.ds(unit, UNITS)], w_local.at[2]),
    ]
    for copy in local:
        copy.start()

    barrier = pltpu.get_barrier_semaphore()
    partners = [sibling]
    partners += [at(0, dy, c) for dy in DY[1:] for c in range(2)]
    partners += [at(dx, 0, c) for dx in (1, -1) for c in range(2)] + [at(2, 0, core)]
    partners += [{"section": above}, {"section": below}]
    for device in partners:
        pl.semaphore_signal(barrier, inc=1, device_id=device, device_id_type=MESH)

    for k in range(8):
        gain_ref[4 * k:4 * k + 4] = jnp.broadcast_to(gain_in[:, Q * k:Q * k + Q], (4, Q))
    for t in range(T):
        for r in range(4):
            ids_f[4 * t + r:4 * t + r + 1] = jnp.broadcast_to(ids_in[t:t + 1, r:r + 1].astype(F32), (1, 128))
            weight = jnp.broadcast_to(1.0 / (1.0 + jnp.exp(-score_in[t:t + 1, r:r + 1])), (1, 128))
            for k in range(8):
                score_ref[t, 4 * k + r:4 * k + r + 1] = weight
    ids_ref[...] = ids_f[...].astype(BF16)

    i = lax.broadcasted_iota(jnp.int32, (256, 256), 0)
    j = lax.broadcasted_iota(jnp.int32, (256, 256), 1)
    perm[...] = jnp.where(
        (i // 64 == (j % 16) // 4) & ((i % 64) // 4 == j // 16) & (i % 4 == j % 4), 1.0, 0.0
    ).astype(BF16)
    perm_t[...] = jnp.where(
        (j // 64 == (i % 16) // 4) & ((j % 64) // 4 == i // 16) & (i % 4 == j % 4), 1.0, 0.0
    ).astype(BF16)
    for a in range(2):
        @pl.when(core == a)
        def _():
            idb[a, 0, 0] = ids_ref[...]

    pl.semaphore_wait(barrier, len(partners))

    remote = [
        (wg_ref.at[pl.ds(other, HALF)], wgu.at[0, :, pl.ds(unit, UNITS)]),
        (wu_ref.at[pl.ds(other, HALF)], wgu.at[1, :, pl.ds(unit, UNITS)]),
        (wd_ref.at[:, pl.ds(other, HALF)], wdn.at[pl.ds(unit, UNITS)]),
    ]

    def place(rows):
        for k in range(8):
            cur[4 * k:4 * k + 4] = rows[:, Q * k:Q * k + Q]

    def spread(t, a):
        @pl.when(core == a)
        def _():
            if not isinstance(t, int):
                @pl.when(section > 0)
                def _():
                    wait(zbuf.at[t], r_z.at[t])
                    cur[...] = zbuf[t].astype(F32)

            if isinstance(t, int):
                place(held_ref[...].astype(F32))
            else:
                @pl.when(section == 0)
                def _():
                    place(arrivals_ref[t - 1].astype(F32))

            wide = cur[...]
            power = jnp.broadcast_to(jnp.sum(wide * wide, axis=1, keepdims=True), (32, 128))
            for shift in (4, 8, 16):
                power = power + pltpu.roll(power, shift, 0)
            scale = lax.rsqrt(power[:, :1] * (1.0 / D) + 1e-05)
            normed = (wide * scale * gain_ref[...]).astype(BF16)
            nb[t, 0] = normed[:16]
            nb[t, 1] = normed[16:]
            for slot in (1, 2):
                for h in range(2):
                    send(nb.at[t, h], ag.at[t, a, 0, INV[slot]], s_own.at[t, 0],
                         r_ag.at[t, a, BATCH_OF[INV[slot]]], at(0, DY[slot], h))
            for h in range(2):
                send(nb.at[t, h], ag.at[t, a, 1, 0], s_own.at[t, 1], r_x.at[t, a, 0, 0], at(1, 0, h))
                send(nb.at[t, h], ag.at[t, a, 2, 0], s_own.at[t, 1], r_x.at[t, a, 1, 0], at(-1, 0, h))
            for slot in range(3, 8):
                for h in range(2):
                    send(nb.at[t, h], ag.at[t, a, 0, INV[slot]], s_own.at[t, 0],
                         r_ag.at[t, a, BATCH_OF[INV[slot]]], at(0, DY[slot], h))
            send(nb.at[t, 1 - core], ag.at[t, a, 0, 0], s_own.at[t, 1], r_ag.at[t, a, 0], sibling)
            ag[t, a, 0, 0] = nb[t, core]

    def along_y(t, a, k):
        first, count = BATCH[k]
        block = ag.at[t, a, 0, pl.ds(first, count)]
        wait(block, r_ag.at[t, a, k])
        send(block, ag.at[t, a, 1, pl.ds(first, count)], s_x.at[t, a, 0], r_x.at[t, a, 0, k], at(1, 0, core))
        send(block, ag.at[t, a, 2, pl.ds(first, count)], s_x.at[t, a, 1], r_x.at[t, a, 1, k], at(-1, 0, core))
        if k == 3:
            send(block, ag.at[t, a, 3, pl.ds(first, count)], s_x2.at[t, a], r_x2.at[t, a], at(2, 0, core))

    def along_x(t, a, k):
        first, count = BATCH[k]
        low = ag.at[t, a, 1, pl.ds(first, count)]
        high = ag.at[t, a, 2, pl.ds(first, count)]
        wait(low, r_x.at[t, a, 0, k])
        wait(high, r_x.at[t, a, 1, k])
        dst = ag.at[t, a, 3, pl.ds(first, count)]
        if k == 0:
            send(low, dst, s_x2.at[t, a], r_x2.at[t, a], at(1, 0, core))
        elif k < 3:
            send(high, dst, s_x2.at[t, a], r_x2.at[t, a], at(-1, 0, core))

    def gate_up(t, a, s):
        if s == 0:
            @pl.when(core != a)
            def _():
                wait(ag.at[t, a, 0, 0], r_ag.at[t, a, 0])
        else:
            wait(ag.at[t, a, 3], r_x2.at[t, a])
        low = 64 * s
        block = ag[t, a, 2 * s:2 * s + 2].reshape(256, Q)
        moved = jnp.dot(perm[...], block, preferred_element_type=F32).astype(BF16)
        rows = jnp.concatenate([moved[64 * q:64 * q + 64] for q in range(4)], axis=1)
        for w in range(2):
            value = jnp.dot(rows, wgu[w], preferred_element_type=F32)
            part[a, low:low + 64, 256 * w:256 * w + 256] = value
            exs[t, a, low:low + 64, 256 * w:256 * w + 256] = value.astype(BF16)
        mine_now = pl.ds(low, 64)
        send(exs.at[t, a, mine_now], exr.at[t, a, mine_now], s_ex.at[t, a, s], r_ex.at[t, a, s], sibling)

    def down(t, a):
        for s in range(2):
            wait(exr.at[t, a, pl.ds(64 * s, 64)], r_ex.at[t, a, s])
        sums = part[a] + exr[t, a].astype(F32)
        gate, up = sums[:, :256], sums[:, 256:]
        keep = mask[t, a]
        hidden = (gate / (1.0 + jnp.exp(-gate)) * up * jnp.concatenate([keep, keep], axis=1)).astype(BF16)
        result = jnp.dot(hidden, wdn[...], preferred_element_type=F32).astype(BF16)
        near, far = pl.ds(0, 4), pl.ds(4, 4)
        for s in (1, 0):
            low = 64 * s
            piece = jnp.concatenate([result[low:low + 64, Q * q:Q * q + Q] for q in range(4)], axis=0)
            moved = jnp.dot(perm_t[...], piece, preferred_element_type=F32).astype(BF16)
            rs[t, a, 2 * s:2 * s + 2] = moved.reshape(2, 8, 16, Q)
            if s:
                send(rs.at[t, a, 3, far], r1.at[t, a, 1], s_rs.at[t, a, 1], r_r1.at[t, a, 1], at(-1, 0, core))
                send(rs.at[t, a, 3, near], r1.at[t, a, 0], s_rs.at[t, a, 0], r_r1.at[t, a, 0], at(1, 0, core))
                send(rs.at[t, a, 2, far], fr.at[t, a, 0, far], s_rs.at[t, a, 2], r_pure.at[t, a, 0], at(1, 0, core))
            else:
                send(rs.at[t, a, 1, near], fr.at[t, a, 1, near], s_rs.at[t, a, 3], r_pure.at[t, a, 1],
                     at(-1, 0, core))

    def relay(t, a, far):
        low = 4 * far
        here, step = (1, -1) if far else (2, 1)
        wait(r1.at[t, a, far], r_r1.at[t, a, far])
        fs[t, a, far] = (rs[t, a, here, low:low + 4].astype(F32) + r1[t, a, far].astype(F32)).astype(BF16)
        send(fs.at[t, a, far], fr.at[t, a, far, pl.ds(low, 4)], s_fs.at[t, a, far], r_sum.at[t, a, far],
             at(step, 0, core))

    def back_y(t, a, far):
        block = pl.ds(4 * far, 4)
        wait(fr.at[t, a, 1 - far, block], r_pure.at[t, a, 1 - far])
        wait(fr.at[t, a, far, block], r_sum.at[t, a, far])
        for slot in range(4 * far + 3, 4 * far - 1, -1):
            ysrc[t, a, slot] = (
                rs[t, a, 0, slot].astype(F32) + fr[t, a, 0, slot].astype(F32) + fr[t, a, 1, slot].astype(F32)
            ).astype(BF16)
            if slot:
                send(ysrc.at[t, a, slot], yr.at[t, core, INV[slot]], s_y.at[t, a, 0], r_y.at[t], at(0, DY[slot], a))
        if not far:
            @pl.when(core == a)
            def _():
                yr[t, core, 0] = ysrc[t, a, 0]

            @pl.when(core != a)
            def _():
                send(ysrc.at[t, a, 0], yr.at[t, core, 0], s_y.at[t, a, 1], r_yc.at[t], sibling)

    def finish(t, a):
        @pl.when(core == a)
        def _():
            wait(yr.at[t, 1 - core, 0], r_yc.at[t])
            wait(yr.at[t, :, pl.ds(1, 7)], r_y.at[t])
            weight = score_ref[t]
            for h in range(2):
                total = yr[t, h, 0].astype(F32)
                for slot in range(1, 8):
                    total = total + yr[t, h, slot].astype(F32)
                value = cur[16 * h:16 * h + 16] + weight[16 * h:16 * h + 16, :1] * total
                zsrc[t, 16 * h:16 * h + 16] = value.astype(BF16)
                for q in range(4):
                    k = 4 * h + q
                    out_ref[t, :, Q * k:Q * k + Q] = value[4 * q:4 * q + 4].astype(BF16)

            @pl.when((t < T - 1) & (section < 7))
            def _():
                send(zsrc.at[t], zbuf.at[t + 1], s_z.at[t], r_z.at[t + 1], {"section": above})

    def masks():
        for a in range(2):
            wait(idb.at[a, 0, pl.ds(1, 7)], id_recv.at[a, 0])

            @pl.when(core != a)
            def _():
                wait(idb.at[a, 0, 0], id_recv.at[a, 1])

            send(idb.at[a, 0], idb.at[a, 1], id_send.at[2 + 3 * a], idx_recv.at[a, 0], at(1, 0, core))
            send(idb.at[a, 0], idb.at[a, 2], id_send.at[3 + 3 * a], idx_recv.at[a, 1], at(-1, 0, core))

    def masks_end():
        for a in range(2):
            wait(idb.at[a, 1], idx_recv.at[a, 0])
            wait(idb.at[a, 2], idx_recv.at[a, 1])
            send(idb.at[a, 1], idb.at[a, 3], id_send.at[4 + 3 * a], idx_recv.at[a, 2], at(1, 0, core))
        expert = lax.div(px, NX // 2).astype(F32)
        for a in range(2):
            wait(idb.at[a, 3], idx_recv.at[a, 2])
            for g in range(2):
                named = jnp.dot(
                    perm[...], idb[a, 2 * g:2 * g + 2].reshape(256, 128), preferred_element_type=F32)
                for t in range(T):
                    mask[t, a, 64 * g:64 * g + 64] = jnp.where(named[64 * t:64 * t + 64] == expert, 1.0, 0.0)

    def start():
        for k, (src, dst) in enumerate(remote):
            send(src, dst, w_send.at[k], w_recv.at[k], sibling)
        for a in range(2):
            @pl.when(core == a)
            def _():
                for slot in range(1, 8):
                    for h in range(2):
                        send(ids_ref, idb.at[a, 0, INV[slot]], id_send.at[0], id_recv.at[a, 0], at(0, DY[slot], h))
                send(ids_ref, idb.at[a, 0, 0], id_send.at[1], id_recv.at[a, 1], sibling)

    def ready():
        for copy in local:
            copy.wait()
        for k, (_, dst) in enumerate(remote):
            wait(dst, w_recv.at[k])

    def drain(t, a):
        for d in range(2):
            wait(ag.at[t, a, 0, pl.ds(1, 7)], s_x.at[t, a, d])
            wait(fs.at[t, a, d], s_fs.at[t, a, d])
            wait(exs.at[t, a, pl.ds(64 * d, 64)], s_ex.at[t, a, d])
        wait(ag.at[t, a, 3], s_x2.at[t, a])
        for k in range(4):
            wait(rs.at[t, a, k, pl.ds(0, 4)], s_rs.at[t, a, k])
        wait(ysrc.at[t, a, pl.ds(1, 7)], s_y.at[t, a, 0])

        @pl.when(core == a)
        def _():
            wait(yr.at[t, :, pl.ds(1, 7)], s_own.at[t, 0])
            wait(yr.at[t, 0, pl.ds(0, 5)], s_own.at[t, 1])

            @pl.when((t < T - 1) & (section < 7))
            def _():
                wait(zsrc.at[t], s_z.at[t])

        @pl.when(core != a)
        def _():
            wait(ysrc.at[t, a, 0], s_y.at[t, a, 1])

    stages = {
        "dr": drain,
        "sp": spread, "fi": finish,
        "y1": lambda t, a: along_y(t, a, 1), "y2": lambda t, a: along_y(t, a, 2), "y3": lambda t, a: along_y(t, a, 3),
        "x0": lambda t, a: along_x(t, a, 0), "x1": lambda t, a: along_x(t, a, 1),
        "x2": lambda t, a: along_x(t, a, 2), "x3": lambda t, a: along_x(t, a, 3),
        "g0": lambda t, a: gate_up(t, a, 0), "g1": lambda t, a: gate_up(t, a, 1),
        "dn": down,
        "rf": lambda t, a: relay(t, a, 1), "rn": lambda t, a: relay(t, a, 0),
        "bf": lambda t, a: back_y(t, a, 1), "bn": lambda t, a: back_y(t, a, 0),
    }

    extra = {"Asp": start, "Ay2": masks, "Ag1": masks_end}

    def tick(t, parts, first=False):
        for name in ORDER:
            late = name.endswith("'")
            if ("late" if late else "now") not in parts:
                continue
            if first and name == "Ag0":
                ready()
            stages[name[1:3]](t - 1 if late else t, "AB".index(name[0]))
            if first and name in extra:
                extra[name]()

    tick(0, ("now",), first=True)

    def later(t, _):
        tick(t, ("now", "late"))
        return 0

    lax.fori_loop(1, T, later, 0)
    tick(T, ("late",))

    for k, (src, _) in enumerate(remote):
        wait(src, w_send.at[k])
    wait(idb.at[:, 0, pl.ds(0, 7)], id_send.at[0])
    wait(ids_ref, id_send.at[1])
    for a in range(2):
        for k in range(3):
            wait(idb.at[a, k], id_send.at[2 + 3 * a + k])


def per_device(held, arrivals, expert_ids, router_scores, norm_gain, w_gate, w_up, w_down):
    vmem, anywhere = pl.BlockSpec(memory_space=pltpu.VMEM), pl.BlockSpec(memory_space=pl.ANY)
    dma = pltpu.SemaphoreType.DMA
    out = pl.pallas_call(
        kernel,
        out_shape=jax.ShapeDtypeStruct((T, 4, D), BF16),
        in_specs=[vmem] * 5 + [anywhere] * 3,
        out_specs=vmem,
        scratch_shapes=[
            pltpu.VMEM((32, Q), F32),
            pltpu.VMEM((16, 128), F32),
            pltpu.VMEM((16, 128), BF16),
            pltpu.VMEM((T, 32, 128), F32),
            pltpu.VMEM((2, HALF, 256), BF16),
            pltpu.VMEM((256, HALF), BF16),
            pltpu.VMEM((256, 256), BF16),
            pltpu.VMEM((256, 256), BF16),
            pltpu.VMEM((32, Q), F32),
            pltpu.VMEM((T, 2, 16, Q), BF16),
            pltpu.VMEM((T, 32, Q), BF16),
            pltpu.VMEM((T, 32, Q), BF16),
            pltpu.VMEM((T, 2, 4, 8, 16, Q), BF16),
            pltpu.VMEM((2, 4, 8, 16, 128), BF16),
            pltpu.VMEM((T, 2, 128, 128), F32),
            pltpu.VMEM((2, 128, 512), F32),
            pltpu.VMEM((T, 2, 128, 512), BF16),
            pltpu.VMEM((T, 2, 128, 512), BF16),
            pltpu.VMEM((T, 2, 4, 8, 16, Q), BF16),
            pltpu.VMEM((T, 2, 2, 4, 16, Q), BF16),
            pltpu.VMEM((T, 2, 2, 8, 16, Q), BF16),
            pltpu.VMEM((T, 2, 2, 4, 16, Q), BF16),
            pltpu.VMEM((T, 2, 8, 16, Q), BF16),
            pltpu.VMEM((T, 2, 8, 16, Q), BF16),
            dma((3,)), dma((3,)), dma((3,)), dma((8,)), dma((2, 2)), dma((2, 3)),
            dma((T, 2)), dma((T, 2, 2)), dma((T, 2)), dma((T, 2, 2)), dma((T, 2, 4)), dma((T, 2, 2)),
            dma((T, 2, 2)), dma((T,)),
            dma((T, 2, 4)), dma((T, 2, 2, 4)), dma((T, 2)), dma((T, 2, 2)), dma((T, 2, 2)), dma((T, 2, 2)),
            dma((T, 2, 2)), dma((T,)), dma((T,)), dma((T,)),
        ],
        compiler_params=pltpu.CompilerParams(
            collective_id=0, has_side_effects=True, vmem_limit_bytes=56 << 20
        ),
        name="relay",
    )(
        held[0], arrivals, norm_gain, expert_ids.reshape(T, 4), router_scores.reshape(T, 4),
        w_gate[0], w_up[0], w_down[0],
    )
    return out.reshape(T, 1, 4, D)


def solution(mesh):
    placed = (
        P("section", "expert", None),
        P(None, "expert", None),
        P(None, "section", "expert", None),
        P(None, "section", "expert"),
        P("section", None),
        P("section", None, "expert"),
        P("section", None, "expert"),
        P("section", "expert", None),
    )
    return jax.shard_map(
        per_device,
        mesh=mesh,
        in_specs=placed,
        out_specs=P(None, "section", "expert", None),
        check_vma=False,
    )
```

```python
import functools

import jax
import jax.numpy as jnp
from jax import lax
from jax.experimental import pallas as pl
from jax.experimental.pallas import tpu as pltpu
from jax.sharding import PartitionSpec as P

MESH = pl.DeviceIdType.MESH
T = 4
NX, NY = 4, 8
D = 5120
HALF = D // 2
Q = HALF // 4
UNITS = 128
DY = (0, 1, -1, 2, -2, 3, -3, 4)
INV = (0, 2, 1, 4, 3, 6, 5, 7)
BATCH = ((0, 1), (1, 2), (3, 2), (5, 3))
BATCH_OF = (0, 1, 1, 2, 2, 3, 3, 3)
ORDER = (
    "Asp", "Bdn'", "Ay1", "Ax0", "Brf'", "Brn'", "Ay2", "Ay3", "Ax1", "Bbf'", "Bbn'",
    "Adr'", "Ax2", "Ax3", "Ag0", "Ag1", "Bfi'", "Bsp", "Adn", "By1", "Bx0", "Arf",
    "Arn", "By2", "By3", "Bx1", "Abf", "Abn", "Bdr'", "Bx2", "Bx3", "Bg0", "Bg1", "Afi",
)
F32, BF16 = jnp.float32, jnp.bfloat16


def kernel(
    held_ref, arrivals_ref, gain_in, ids_in, score_in, wg_ref, wu_ref, wd_ref, out_ref,
    gain_ref, ids_f, ids_ref, score_ref, wgu, wdn, perm, perm_t, cur, nb, zbuf, zsrc, ag, idb, mask, part, exs, exr,
    rs, r1, fr, fs, ysrc, yr,
    w_send, w_recv, w_local, id_send, id_recv, idx_recv,
    s_own, s_x, s_x2, s_ex, s_rs, s_fs, s_y, s_z,
    r_ag, r_x, r_x2, r_ex, r_r1, r_pure, r_sum, r_y, r_yc, r_z,
):
    section = lax.axis_index("section")
    me = lax.axis_index("expert")
    core = lax.rem(me, 2)
    chip = lax.div(me, 2)
    py = lax.rem(chip, NY)
    px = lax.div(chip, NY)
    chips = {(0, dy): (px * NY + lax.rem(py + dy + NY, NY)) * 2 for dy in DY}
    chips.update({(dx, 0): (lax.rem(px + dx + NX, NX) * NY + py) * 2 for dx in (1, -1, 2)})
    above, below = lax.rem(section + 1, 8), lax.rem(section + 7, 8)

    def at(dx, dy, c):
        return {"expert": chips[dx, dy] + c}

    sibling = at(0, 0, 1 - core)

    def send(src, dst, send_sem, recv_sem, device):
        pltpu.make_async_remote_copy(
            src_ref=src, dst_ref=dst, send_sem=send_sem, recv_sem=recv_sem,
            device_id=device, device_id_type=MESH,
        ).start()

    def wait(ref, sem):
        pltpu.make_async_copy(ref, ref, sem).wait()

    mine = pl.multiple_of(core * HALF, HALF)
    other = pl.multiple_of((1 - core) * HALF, HALF)
    unit = pl.multiple_of(core * UNITS, UNITS)
    local = [
        pltpu.make_async_copy(
            wg_ref.at[pl.ds(mine, HALF)], wgu.at[0, :, pl.ds(unit, UNITS)], w_local.at[0]),
        pltpu.make_async_copy(
            wu_ref.at[pl.ds(mine, HALF)], wgu.at[1, :, pl.ds(unit, UNITS)], w_local.at[1]),
        pltpu.make_async_copy(
            wd_ref.at[:, pl.ds(mine, HALF)], wdn.at[pl.ds(unit, UNITS)], w_local.at[2]),
    ]
    for copy in local:
        copy.start()

    barrier = pltpu.get_barrier_semaphore()
    partners = [sibling]
    partners += [at(0, dy, c) for dy in DY[1:] for c in range(2)]
    partners += [at(dx, 0, c) for dx in (1, -1) for c in range(2)] + [at(2, 0, core)]
    partners += [{"section": above}, {"section": below}]
    for device in partners:
        pl.semaphore_signal(barrier, inc=1, device_id=device, device_id_type=MESH)

    for k in range(8):
        gain_ref[4 * k:4 * k + 4] = jnp.broadcast_to(gain_in[:, Q * k:Q * k + Q], (4, Q))
    for t in range(T):
        for r in range(4):
            ids_f[4 * t + r:4 * t + r + 1] = jnp.broadcast_to(ids_in[t:t + 1, r:r + 1].astype(F32), (1, 128))
            weight = jnp.broadcast_to(1.0 / (1.0 + jnp.exp(-score_in[t:t + 1, r:r + 1])), (1, 128))
            for k in range(8):
                score_ref[t, 4 * k + r:4 * k + r + 1] = weight
    ids_ref[...] = ids_f[...].astype(BF16)

    i = lax.broadcasted_iota(jnp.int32, (256, 256), 0)
    j = lax.broadcasted_iota(jnp.int32, (256, 256), 1)
    perm[...] = jnp.where(
        (i // 64 == (j % 16) // 4) & ((i % 64) // 4 == j // 16) & (i % 4 == j % 4), 1.0, 0.0
    ).astype(BF16)
    perm_t[...] = jnp.where(
        (j // 64 == (i % 16) // 4) & ((j % 64) // 4 == i // 16) & (i % 4 == j % 4), 1.0, 0.0
    ).astype(BF16)
    for a in range(2):
        @pl.when(core == a)
        def _():
            idb[a, 0, 0] = ids_ref[...]

    pl.semaphore_wait(barrier, len(partners))

    remote = [
        (wg_ref.at[pl.ds(other, HALF)], wgu.at[0, :, pl.ds(unit, UNITS)]),
        (wu_ref.at[pl.ds(other, HALF)], wgu.at[1, :, pl.ds(unit, UNITS)]),
        (wd_ref.at[:, pl.ds(other, HALF)], wdn.at[pl.ds(unit, UNITS)]),
    ]

    def place(rows):
        for k in range(8):
            cur[4 * k:4 * k + 4] = rows[:, Q * k:Q * k + Q]

    def spread(t, a):
        @pl.when(core == a)
        def _():
            if not isinstance(t, int):
                @pl.when(section > 0)
                def _():
                    wait(zbuf.at[t], r_z.at[t])
                    cur[...] = zbuf[t].astype(F32)

            if isinstance(t, int):
                place(held_ref[...].astype(F32))
            else:
                @pl.when(section == 0)
                def _():
                    place(arrivals_ref[t - 1].astype(F32))

            wide = cur[...]
            power = jnp.broadcast_to(jnp.sum(wide * wide, axis=1, keepdims=True), (32, 128))
            for shift in (4, 8, 16):
                power = power + pltpu.roll(power, shift, 0)
            scale = lax.rsqrt(power[:, :1] * (1.0 / D) + 1e-05)
            normed = (wide * scale * gain_ref[...]).astype(BF16)
            nb[t, 0] = normed[:16]
            nb[t, 1] = normed[16:]
            for slot in (1, 2):
                for h in range(2):
                    send(nb.at[t, h], ag.at[t, a, 0, INV[slot]], s_own.at[t, 0],
                         r_ag.at[t, a, BATCH_OF[INV[slot]]], at(0, DY[slot], h))
            for h in range(2):
                send(nb.at[t, h], ag.at[t, a, 1, 0], s_own.at[t, 1], r_x.at[t, a, 0, 0], at(1, 0, h))
                send(nb.at[t, h], ag.at[t, a, 2, 0], s_own.at[t, 1], r_x.at[t, a, 1, 0], at(-1, 0, h))
            for slot in range(3, 8):
                for h in range(2):
                    send(nb.at[t, h], ag.at[t, a, 0, INV[slot]], s_own.at[t, 0],
                         r_ag.at[t, a, BATCH_OF[INV[slot]]], at(0, DY[slot], h))
            send(nb.at[t, 1 - core], ag.at[t, a, 0, 0], s_own.at[t, 1], r_ag.at[t, a, 0], sibling)
            ag[t, a, 0, 0] = nb[t, core]

    def along_y(t, a, k):
        first, count = BATCH[k]
        block = ag.at[t, a, 0, pl.ds(first, count)]
        wait(block, r_ag.at[t, a, k])
        send(block, ag.at[t, a, 1, pl.ds(first, count)], s_x.at[t, a, 0], r_x.at[t, a, 0, k], at(1, 0, core))
        send(block, ag.at[t, a, 2, pl.ds(first, count)], s_x.at[t, a, 1], r_x.at[t, a, 1, k], at(-1, 0, core))
        if k == 3:
            send(block, ag.at[t, a, 3, pl.ds(first, count)], s_x2.at[t, a], r_x2.at[t, a], at(2, 0, core))

    def along_x(t, a, k):
        first, count = BATCH[k]
        low = ag.at[t, a, 1, pl.ds(first, count)]
        high = ag.at[t, a, 2, pl.ds(first, count)]
        wait(low, r_x.at[t, a, 0, k])
        wait(high, r_x.at[t, a, 1, k])
        dst = ag.at[t, a, 3, pl.ds(first, count)]
        if k == 0:
            send(low, dst, s_x2.at[t, a], r_x2.at[t, a], at(1, 0, core))
        elif k < 3:
            send(high, dst, s_x2.at[t, a], r_x2.at[t, a], at(-1, 0, core))

    def gate_up(t, a, s):
        if s == 0:
            @pl.when(core != a)
            def _():
                wait(ag.at[t, a, 0, 0], r_ag.at[t, a, 0])
        else:
            wait(ag.at[t, a, 3], r_x2.at[t, a])
        low = 64 * s
        block = ag[t, a, 2 * s:2 * s + 2].reshape(256, Q)
        moved = jnp.dot(perm[...], block, preferred_element_type=F32).astype(BF16)
        rows = jnp.concatenate([moved[64 * q:64 * q + 64] for q in range(4)], axis=1)
        for w in range(2):
            value = jnp.dot(rows, wgu[w], preferred_element_type=F32)
            part[a, low:low + 64, 256 * w:256 * w + 256] = value
            exs[t, a, low:low + 64, 256 * w:256 * w + 256] = value.astype(BF16)
        mine_now = pl.ds(low, 64)
        send(exs.at[t, a, mine_now], exr.at[t, a, mine_now], s_ex.at[t, a, s], r_ex.at[t, a, s], sibling)

    def down(t, a):
        for s in range(2):
            wait(exr.at[t, a, pl.ds(64 * s, 64)], r_ex.at[t, a, s])
        sums = part[a] + exr[t, a].astype(F32)
        gate, up = sums[:, :256], sums[:, 256:]
        keep = mask[t, a]
        hidden = (gate / (1.0 + jnp.exp(-gate)) * up * jnp.concatenate([keep, keep], axis=1)).astype(BF16)
        result = jnp.dot(hidden, wdn[...], preferred_element_type=F32).astype(BF16)
        near, far = pl.ds(0, 4), pl.ds(4, 4)
        for s in (1, 0):
            low = 64 * s
            piece = jnp.concatenate([result[low:low + 64, Q * q:Q * q + Q] for q in range(4)], axis=0)
            moved = jnp.dot(perm_t[...], piece, preferred_element_type=F32).astype(BF16)
            rs[t, a, 2 * s:2 * s + 2] = moved.reshape(2, 8, 16, Q)
            if s:
                send(rs.at[t, a, 3, far], r1.at[t, a, 1], s_rs.at[t, a, 1], r_r1.at[t, a, 1], at(-1, 0, core))
                send(rs.at[t, a, 3, near], r1.at[t, a, 0], s_rs.at[t, a, 0], r_r1.at[t, a, 0], at(1, 0, core))
                send(rs.at[t, a, 2, far], fr.at[t, a, 0, far], s_rs.at[t, a, 2], r_pure.at[t, a, 0], at(1, 0, core))
            else:
                send(rs.at[t, a, 1, near], fr.at[t, a, 1, near], s_rs.at[t, a, 3], r_pure.at[t, a, 1],
                     at(-1, 0, core))

    def relay(t, a, far):
        low = 4 * far
        here, step = (1, -1) if far else (2, 1)
        wait(r1.at[t, a, far], r_r1.at[t, a, far])
        fs[t, a, far] = (rs[t, a, here, low:low + 4].astype(F32) + r1[t, a, far].astype(F32)).astype(BF16)
        send(fs.at[t, a, far], fr.at[t, a, far, pl.ds(low, 4)], s_fs.at[t, a, far], r_sum.at[t, a, far],
             at(step, 0, core))

    def back_y(t, a, far):
        block = pl.ds(4 * far, 4)
        wait(fr.at[t, a, 1 - far, block], r_pure.at[t, a, 1 - far])
        wait(fr.at[t, a, far, block], r_sum.at[t, a, far])
        for slot in range(4 * far + 3, 4 * far - 1, -1):
            ysrc[t, a, slot] = (
                rs[t, a, 0, slot].astype(F32) + fr[t, a, 0, slot].astype(F32) + fr[t, a, 1, slot].astype(F32)
            ).astype(BF16)
            if slot:
                send(ysrc.at[t, a, slot], yr.at[t, core, INV[slot]], s_y.at[t, a, 0], r_y.at[t], at(0, DY[slot], a))
        if not far:
            @pl.when(core == a)
            def _():
                yr[t, core, 0] = ysrc[t, a, 0]

            @pl.when(core != a)
            def _():
                send(ysrc.at[t, a, 0], yr.at[t, core, 0], s_y.at[t, a, 1], r_yc.at[t], sibling)

    def finish(t, a):
        @pl.when(core == a)
        def _():
            wait(yr.at[t, 1 - core, 0], r_yc.at[t])
            wait(yr.at[t, :, pl.ds(1, 7)], r_y.at[t])
            weight = score_ref[t]
            values = []
            for h in range(2):
                total = yr[t, h, 0].astype(F32)
                for slot in range(1, 8):
                    total = total + yr[t, h, slot].astype(F32)
                part_of = pl.ds(16 * h, 16)
                value = (cur[16 * h:16 * h + 16] + weight[16 * h:16 * h + 16, :1] * total).astype(BF16)
                zsrc[t, 16 * h:16 * h + 16] = value
                values.append(value)

                @pl.when((t < T - 1) & (section < 7))
                def _():
                    send(zsrc.at[t, part_of], zbuf.at[t + 1, part_of], s_z.at[t], r_z.at[t + 1], {"section": above})

            for k in range(8):
                row = 4 * (k % 4)
                out_ref[t, :, Q * k:Q * k + Q] = values[k // 4].astype(F32)[row:row + 4].astype(BF16)

    def masks():
        for a in range(2):
            wait(idb.at[a, 0, pl.ds(1, 7)], id_recv.at[a, 0])

            @pl.when(core != a)
            def _():
                wait(idb.at[a, 0, 0], id_recv.at[a, 1])

            send(idb.at[a, 0], idb.at[a, 1], id_send.at[2 + 3 * a], idx_recv.at[a, 0], at(1, 0, core))
            send(idb.at[a, 0], idb.at[a, 2], id_send.at[3 + 3 * a], idx_recv.at[a, 1], at(-1, 0, core))

    def masks_end():
        for a in range(2):
            wait(idb.at[a, 1], idx_recv.at[a, 0])
            wait(idb.at[a, 2], idx_recv.at[a, 1])
            send(idb.at[a, 1], idb.at[a, 3], id_send.at[4 + 3 * a], idx_recv.at[a, 2], at(1, 0, core))
        expert = lax.div(px, NX // 2).astype(F32)
        for a in range(2):
            wait(idb.at[a, 3], idx_recv.at[a, 2])
            for g in range(2):
                named = jnp.dot(
                    perm[...], idb[a, 2 * g:2 * g + 2].reshape(256, 128), preferred_element_type=F32)
                for t in range(T):
                    mask[t, a, 64 * g:64 * g + 64] = jnp.where(named[64 * t:64 * t + 64] == expert, 1.0, 0.0)

    def start():
        for k, (src, dst) in enumerate(remote):
            send(src, dst, w_send.at[k], w_recv.at[k], sibling)
        for a in range(2):
            @pl.when(core == a)
            def _():
                for slot in range(1, 8):
                    for h in range(2):
                        send(ids_ref, idb.at[a, 0, INV[slot]], id_send.at[0], id_recv.at[a, 0], at(0, DY[slot], h))
                send(ids_ref, idb.at[a, 0, 0], id_send.at[1], id_recv.at[a, 1], sibling)

    def ready():
        for copy in local:
            copy.wait()
        for k, (_, dst) in enumerate(remote):
            wait(dst, w_recv.at[k])

    def drain(t, a):
        for d in range(2):
            wait(ag.at[t, a, 0, pl.ds(1, 7)], s_x.at[t, a, d])
            wait(fs.at[t, a, d], s_fs.at[t, a, d])
            wait(exs.at[t, a, pl.ds(64 * d, 64)], s_ex.at[t, a, d])
        wait(ag.at[t, a, 3], s_x2.at[t, a])
        for k in range(4):
            wait(rs.at[t, a, k, pl.ds(0, 4)], s_rs.at[t, a, k])
        wait(ysrc.at[t, a, pl.ds(1, 7)], s_y.at[t, a, 0])

        @pl.when(core == a)
        def _():
            wait(yr.at[t, :, pl.ds(1, 7)], s_own.at[t, 0])
            wait(yr.at[t, 0, pl.ds(0, 5)], s_own.at[t, 1])

            @pl.when((t < T - 1) & (section < 7))
            def _():
                wait(zsrc.at[t], s_z.at[t])

        @pl.when(core != a)
        def _():
            wait(ysrc.at[t, a, 0], s_y.at[t, a, 1])

    stages = {
        "dr": drain,
        "sp": spread, "fi": finish,
        "y1": lambda t, a: along_y(t, a, 1), "y2": lambda t, a: along_y(t, a, 2), "y3": lambda t, a: along_y(t, a, 3),
        "x0": lambda t, a: along_x(t, a, 0), "x1": lambda t, a: along_x(t, a, 1),
        "x2": lambda t, a: along_x(t, a, 2), "x3": lambda t, a: along_x(t, a, 3),
        "g0": lambda t, a: gate_up(t, a, 0), "g1": lambda t, a: gate_up(t, a, 1),
        "dn": down,
        "rf": lambda t, a: relay(t, a, 1), "rn": lambda t, a: relay(t, a, 0),
        "bf": lambda t, a: back_y(t, a, 1), "bn": lambda t, a: back_y(t, a, 0),
    }

    extra = {"Asp": start, "Ay2": masks, "Ag1": masks_end}

    def tick(t, parts, first=False):
        for name in ORDER:
            late = name.endswith("'")
            if ("late" if late else "now") not in parts:
                continue
            if first and name == "Ag0":
                ready()
            stages[name[1:3]](t - 1 if late else t, "AB".index(name[0]))
            if first and name in extra:
                extra[name]()

    tick(0, ("now",), first=True)

    def later(t, _):
        tick(t, ("now", "late"))
        return 0

    lax.fori_loop(1, T, later, 0)
    tick(T, ("late",))

    for k, (src, _) in enumerate(remote):
        wait(src, w_send.at[k])
    wait(idb.at[:, 0, pl.ds(0, 7)], id_send.at[0])
    wait(ids_ref, id_send.at[1])
    for a in range(2):
        for k in range(3):
            wait(idb.at[a, k], id_send.at[2 + 3 * a + k])


def per_device(held, arrivals, expert_ids, router_scores, norm_gain, w_gate, w_up, w_down):
    vmem, anywhere = pl.BlockSpec(memory_space=pltpu.VMEM), pl.BlockSpec(memory_space=pl.ANY)
    dma = pltpu.SemaphoreType.DMA
    out = pl.pallas_call(
        kernel,
        out_shape=jax.ShapeDtypeStruct((T, 4, D), BF16),
        in_specs=[vmem] * 5 + [anywhere] * 3,
        out_specs=vmem,
        scratch_shapes=[
            pltpu.VMEM((32, Q), F32),
            pltpu.VMEM((16, 128), F32),
            pltpu.VMEM((16, 128), BF16),
            pltpu.VMEM((T, 32, 128), F32),
            pltpu.VMEM((2, HALF, 256), BF16),
            pltpu.VMEM((256, HALF), BF16),
            pltpu.VMEM((256, 256), BF16),
            pltpu.VMEM((256, 256), BF16),
            pltpu.VMEM((32, Q), F32),
            pltpu.VMEM((T, 2, 16, Q), BF16),
            pltpu.VMEM((T, 32, Q), BF16),
            pltpu.VMEM((T, 32, Q), BF16),
            pltpu.VMEM((T, 2, 4, 8, 16, Q), BF16),
            pltpu.VMEM((2, 4, 8, 16, 128), BF16),
            pltpu.VMEM((T, 2, 128, 128), F32),
            pltpu.VMEM((2, 128, 512), F32),
            pltpu.VMEM((T, 2, 128, 512), BF16),
            pltpu.VMEM((T, 2, 128, 512), BF16),
            pltpu.VMEM((T, 2, 4, 8, 16, Q), BF16),
            pltpu.VMEM((T, 2, 2, 4, 16, Q), BF16),
            pltpu.VMEM((T, 2, 2, 8, 16, Q), BF16),
            pltpu.VMEM((T, 2, 2, 4, 16, Q), BF16),
            pltpu.VMEM((T, 2, 8, 16, Q), BF16),
            pltpu.VMEM((T, 2, 8, 16, Q), BF16),
            dma((3,)), dma((3,)), dma((3,)), dma((8,)), dma((2, 2)), dma((2, 3)),
            dma((T, 2)), dma((T, 2, 2)), dma((T, 2)), dma((T, 2, 2)), dma((T, 2, 4)), dma((T, 2, 2)),
            dma((T, 2, 2)), dma((T,)),
            dma((T, 2, 4)), dma((T, 2, 2, 4)), dma((T, 2)), dma((T, 2, 2)), dma((T, 2, 2)), dma((T, 2, 2)),
            dma((T, 2, 2)), dma((T,)), dma((T,)), dma((T,)),
        ],
        compiler_params=pltpu.CompilerParams(
            collective_id=0, has_side_effects=True, vmem_limit_bytes=56 << 20
        ),
        name="relay",
    )(
        held[0], arrivals, norm_gain, expert_ids.reshape(T, 4), router_scores.reshape(T, 4),
        w_gate[0], w_up[0], w_down[0],
    )
    return out.reshape(T, 1, 4, D)


def solution(mesh):
    placed = (
        P("section", "expert", None),
        P(None, "expert", None),
        P(None, "section", "expert", None),
        P(None, "section", "expert"),
        P("section", None),
        P("section", None, "expert"),
        P("section", None, "expert"),
        P("section", "expert", None),
    )
    return jax.shard_map(
        per_device,
        mesh=mesh,
        in_specs=placed,
        out_specs=P(None, "section", "expert", None),
        check_vma=False,
    )
```
